32 devices in a mesh: groups: 2 (over x), shard: 16 (over z, y, core).
Axes of the slice: x: 2, y: 2, z: 4, core: 2. Of those that a mesh axis runs over, the one named last changes fastest.
Arguments:
- hidden: bfloat16 [8192, 8192], P(('groups', 'shard')), parts along dimension 0, may hold values from -6 to 6
- queries: bfloat16 [8192, 4096], P(('groups', 'shard')), parts along dimension 0, may hold values from -48 to 48
- segment: int32 [8192], P('groups'), parts along dimension 0, may hold values from 0 to 4095, as said below
- target_device: int32 [32], P('groups'), parts along dimension 0, may hold values from 0 to 15, as said below
- target_slot: int32 [32], P('groups'), parts along dimension 0, may hold values from 0 to 1, as said below
- key_codes: bfloat16 [8192, 512], P('shard'), may hold values from -0.0625 to 0.0625
- key_scales: float32 [64, 4], P('shard'), may hold values from 0.5 to 2
- value_codes: bfloat16 [8192, 512], P('shard'), may hold values from -0.0625 to 0.0625
- value_scales: float32 [64, 4], P('shard'), may hold values from 0.5 to 2
Outputs:
- attended: bfloat16 [16384, 4096], P(('groups', 'shard')), parts along dimension 0
The draws below stay inside these ranges and needn't reach their ends.
There are 2 independent parts, one for each index of `groups`. The reference program is written for one: setup_inputs(seed, part) draws one part's arguments, and reference() takes and returns one part's arrays. A program takes and returns all parts, laid end to end along the dimension named above; an argument that names none is the same for every part. Nothing has to cross between parts.
Inputs may be any that keep to these rules, and one draw needn't show every extreme that they name: Block b, the 256 rows that shard index b holds, goes to shard index target_device[b], at most 1 places away counting cyclically. The blocks of one rollout all go to one device, in their cyclic order, to slots 0, 1, and so on; a device receives at most 2 blocks and at most one from each device. In every draw some device receives 2 blocks, and every displacement from -1 to 1 occurs. `target_slot`: blocks with one destination have distinct slots. `segment`: ids are distinct between rollouts, and both ends of the range occur in every draw. A rollout's rows lie in blocks that go to one device, in slot order then row order; a rollout has at most 512 rows, and one has that many in every draw.
All inputs are finite; a program needn't handle non-finite values.
Results may differ from the reference program's by a relative error of at most 0.012.
The reference program's roundings to bfloat16 on the way (of `key_weight`, `value_weight`, `keys`, `values` and `weights`) count: a program that leaves them out, or rounds other values in their place, can miss the bound.
Values may be sent and summed in bfloat16 or wider, within the bound.
A program may use at most 192 MiB of HBM per device.

```python
import math
import jax
import jax.numpy as jnp
from jax import lax

D = 8192
KVH = 4
HD = 128
QPK = 8
QB = 128
BLOCK = 256
CAP = 2
HOP = 1
KVW = 512
QW = 4096
TOKENS = 4096
N_SHARD = 16


def layout(key):
    cycle_size = N_SHARD
    key_size, key_offset, key_turn, key_cut = jax.random.split(key, 4)
    raw_sizes = jax.random.randint(key_size, (cycle_size,), 1, CAP + 1)
    places = jnp.arange(cycle_size)
    sizes = jnp.where(places < 2, CAP, raw_sizes)
    starts = jnp.cumsum(sizes) - sizes
    ends = jnp.minimum(starts + sizes, cycle_size)
    owner = jnp.sum((starts[None, :] <= places[:, None]).astype(jnp.int32), axis=1) - 1
    start_place = starts[owner]
    size_place = ends[owner] - start_place
    lowest = jnp.maximum(0, size_place - 1 - HOP)
    highest = jnp.minimum(size_place - 1, HOP)
    picks = jax.random.randint(key_offset, (cycle_size,), 0, 1 << 20)
    drawn_offset = lowest + picks[owner] % (highest - lowest + 1)
    offset = jnp.where(owner == 0, lowest, jnp.where(owner == 1, highest, drawn_offset))
    turn = jax.random.randint(key_turn, (), 0, cycle_size)
    dest_place = (start_place + offset + turn) % cycle_size
    slot_place = places - start_place
    source = (places - turn) % cycle_size
    row_total = cycle_size * BLOCK
    row_place = jnp.arange(row_total)
    block_place = row_place // BLOCK
    spacing = max(BLOCK // 8, 1)
    begins = jnp.logical_and(row_place % BLOCK == 0, start_place[block_place] == block_place)
    coins = jax.random.randint(key_cut, (row_total,), 0, 6)
    cuts = jnp.logical_and(jnp.logical_and(row_place % spacing == 0, coins == 0), owner[block_place] > 0)
    segment_place = jnp.cumsum(jnp.logical_or(begins, cuts).astype(jnp.int32)) - 1
    counts = jax.ops.segment_sum(jnp.ones((row_total,), jnp.int32), segment_place, num_segments=row_total)
    last_rows = jnp.cumsum(counts) - 1
    segment_ids = jnp.where(segment_place == 0, 0, last_rows[segment_place])
    segment_rows = segment_ids.reshape(cycle_size, BLOCK)[source].reshape(-1)
    return (dest_place[source].astype(jnp.int32), slot_place[source].astype(jnp.int32), segment_rows.astype(jnp.int32))


def draw_target_device(key, part):
    shared = layout(key)
    return shared[0]


def draw_target_slot(key, part):
    shared = layout(key)
    return shared[1]


def draw_segment(key, part):
    shared = layout(key)
    return shared[2]


def draw_queries(key, part):
    key = jax.random.fold_in(key, 5)
    return jnp.clip(jax.random.normal(key, (TOKENS, QW), jnp.float32), -6.0, 6.0).astype(jnp.bfloat16)


def block_levels(key, dims, cuts, least, top_value):
    factor_of, own = 1.0, jax.random.fold_in(key, 6)
    for position, parts in cuts:
        draws = jnp.exp(jax.random.uniform(jax.random.fold_in(own, position), (parts,), jnp.float32, least / len(cuts), top_value / len(cuts)))
        factor_of = factor_of * jnp.repeat(draws, dims[position] // parts).reshape([-1 if axis == position else 1 for axis in range(len(dims))])
    return factor_of


def normal_values(stream_key, shape, deviation, most, cuts=(), kind=jnp.bfloat16):
    values = jax.random.normal(stream_key, shape, jnp.float32) * deviation
    if len(cuts) > 0:
        values = block_levels(stream_key, shape, cuts, -0.22, 0.18) * values
    return jnp.clip(values, min=-most, max=most).astype(kind)


def setup_inputs(seed: int = 0, part: int = 0) -> dict:
    arg_keys = jax.random.split(jax.random.key(seed), 10)
    part_splits = jax.random.split(jax.random.fold_in(arg_keys[9], part), 10)
    hidden = normal_values(part_splits[0], (TOKENS, D), 1.0, 6.0, ((0, 16),))
    queries = draw_queries(jax.random.fold_in(jax.random.fold_in(arg_keys[9], part), 71), part)
    segment = draw_segment(jax.random.fold_in(jax.random.fold_in(arg_keys[9], part), 71), part)
    target_device = draw_target_device(jax.random.fold_in(jax.random.fold_in(arg_keys[9], part), 71), part)
    target_slot = draw_target_slot(jax.random.fold_in(jax.random.fold_in(arg_keys[9], part), 71), part)
    key_codes = normal_values(arg_keys[5], (D, KVW), D ** -0.5, 0.0625, ((0, 16),))
    key_scales = jnp.clip(jnp.exp(math.log(2.0) - 1.3862944 * jax.random.uniform(arg_keys[6], (D // QB, KVW // QB), jnp.float32) ** block_levels(arg_keys[6], (D // QB, KVW // QB), ((0, 16),), -0.2, 0.2)), 0.5, 2.0)
    value_codes = normal_values(arg_keys[7], (D, KVW), D ** -0.5, 0.0625, ((0, 16),))
    value_scales = jnp.clip(jnp.exp(math.log(2.0) - 1.3862944 * jax.random.uniform(arg_keys[8], (D // QB, KVW // QB), jnp.float32) ** block_levels(arg_keys[8], (D // QB, KVW // QB), ((0, 16),), -0.2, 0.2)), 0.5, 2.0)
    return dict(hidden=hidden, queries=queries, segment=segment, target_device=target_device, target_slot=target_slot, key_codes=key_codes, key_scales=key_scales, value_codes=value_codes, value_scales=value_scales)


def dequantize(codes, scales):
    row_count, col_count = codes.shape
    blocks = codes.astype(jnp.float32).reshape(row_count // QB, QB, col_count // QB, QB)
    scaled = blocks * scales[:, None, :, None]
    return scaled.reshape(row_count, col_count).astype(jnp.bfloat16)


def attend_device(operands):
    query_rows, key_rows, value_rows, segment_rows = operands
    total_rows = query_rows.shape[0]
    query_heads = query_rows.astype(jnp.float32).reshape(total_rows, KVH, QPK, HD)
    key_heads = key_rows.astype(jnp.float32).reshape(total_rows, KVH, HD)
    value_heads = value_rows.astype(jnp.float32).reshape(total_rows, KVH, HD)
    scores = jnp.einsum("rgqd,sgd->gqrs", query_heads, key_heads) * (HD ** -0.5)
    positions = jnp.arange(total_rows, dtype=jnp.int32)
    allowed = jnp.logical_and(segment_rows[:, None] == segment_rows[None, :], positions[None, :] <= positions[:, None])
    masked = jnp.where(allowed, scores, -1e30)
    row_max = jnp.max(masked, axis=-1, keepdims=True)
    raised = jnp.where(allowed, jnp.exp(masked - row_max), 0.0)
    weights = (raised / jnp.sum(raised, axis=-1, keepdims=True)).astype(jnp.bfloat16)
    mixed_rows = jnp.einsum("gqrs,sgd->rgqd", weights.astype(jnp.float32), value_heads)
    result = mixed_rows.reshape(total_rows, KVH * QPK * HD).astype(jnp.bfloat16)
    return jnp.where(segment_rows[:, None] >= 0, result, jnp.zeros_like(result))


def reference(hidden, queries, segment, target_device, target_slot, key_codes, key_scales, value_codes, value_scales):
    key_weight = dequantize(key_codes, key_scales)
    value_weight = dequantize(value_codes, value_scales)
    keys = jnp.dot(hidden, key_weight, preferred_element_type=jnp.float32).astype(jnp.bfloat16)
    values = jnp.dot(hidden, value_weight, preferred_element_type=jnp.float32).astype(jnp.bfloat16)
    within = jnp.arange(BLOCK, dtype=jnp.int32)
    starts = (target_device.astype(jnp.int32) * CAP + target_slot.astype(jnp.int32)) * BLOCK
    target_rows = (starts[:, None] + within[None, :]).reshape(-1).astype(jnp.int32)
    slot_total = N_SHARD * CAP * BLOCK
    slot_keys = jnp.zeros((slot_total, keys.shape[1]), jnp.bfloat16).at[target_rows].set(keys)
    slot_values = jnp.zeros((slot_total, values.shape[1]), jnp.bfloat16).at[target_rows].set(values)
    slot_queries = jnp.zeros((slot_total, queries.shape[1]), jnp.bfloat16).at[target_rows].set(queries)
    slot_segment = jnp.full((slot_total,), -1, jnp.int32).at[target_rows].set(segment.astype(jnp.int32))
    device_rows = CAP * BLOCK
    stacked = lax.map(attend_device, (slot_queries.reshape(N_SHARD, device_rows, -1), slot_keys.reshape(N_SHARD, device_rows, -1), slot_values.reshape(N_SHARD, device_rows, -1), slot_segment.reshape(N_SHARD, device_rows)))
    return stacked.reshape(slot_total, -1)
```

```python
import jax
import jax.numpy as jnp
from jax import lax
from jax.experimental import pallas as pl
from jax.experimental.pallas import tpu as pltpu
from jax.sharding import PartitionSpec as P

KVH = 4
HD = 128
QPK = 8
QB = 128
CAP = 2
HOP = 1
LOG2E = 1.4426950408889634


def passed_along(block, axis, distance):
    devices = range(lax.axis_size(axis))
    route = [((i - distance) % len(devices), i) for i in devices]
    return lax.ppermute(block, axis, route)


def dequantize(codes, scales):
    row_count, col_count = codes.shape
    blocks = codes.astype(jnp.float32).reshape(row_count // QB, QB, col_count // QB, QB)
    scaled = blocks * scales[:, None, :, None]
    return scaled.reshape(row_count, col_count).astype(jnp.bfloat16)


def regroup(payload, target_device, target_slot):
    cycle_size = lax.axis_size("shard")
    own_index = lax.axis_index("shard")
    slot_ids = jnp.arange(CAP, dtype=jnp.int32)
    result = jnp.zeros((CAP,) + payload.shape, payload.dtype)
    for offset in range(-HOP, HOP + 1):
        if offset == 0:
            arrived = payload
        else:
            arrived = passed_along(payload, "shard", offset)
        source = (own_index - offset) % cycle_size
        landing = lax.dynamic_index_in_dim(target_device, source, keepdims=False) == own_index
        wanted = lax.dynamic_index_in_dim(target_slot, source, keepdims=False)
        chosen = jnp.logical_and(slot_ids == wanted, landing)
        result = jnp.where(chosen[:, None, None], arrived[None], result)
    return result.reshape(CAP * payload.shape[0], payload.shape[1])


def slot_segments(segment, target_device, target_slot):
    own_index = lax.axis_index("shard")
    block_count = target_device.shape[0]
    segment_rows = segment.reshape(block_count, -1)
    matches = jnp.logical_and(
        target_device[:, None] == own_index,
        target_slot[:, None] == jnp.arange(CAP, dtype=jnp.int32)[None, :],
    )
    summed = jnp.sum(jnp.where(matches[:, :, None], segment_rows[:, None, :], 0), axis=0)
    present = jnp.any(matches, axis=0)
    return jnp.where(present[:, None], summed, -1).reshape(-1)


def projector(hidden_rows, portion):
    return jnp.dot(hidden_rows, portion, preferred_element_type=jnp.float32)


def attention_kernel(row_seg_ref, col_seg_ref, q_ref, k_ref, v_ref, out_ref, bias_ref):
    rows = q_ref.shape[0]
    half = rows // CAP
    factor = HD ** (-0.5) * LOG2E

    @pl.when(pl.program_id(0) == 0)
    def _():
        row_index = lax.broadcasted_iota(jnp.int32, (rows, rows), 0)
        col_index = lax.broadcasted_iota(jnp.int32, (rows, rows), 1)
        allowed = jnp.logical_and(row_seg_ref[...] == col_seg_ref[...], col_index <= row_index)
        bias_ref[...] = jnp.where(allowed, 0.0, -1e30)

    ones = jnp.ones((rows, HD), jnp.bfloat16)
    v_wide = jnp.concatenate([v_ref[...], ones], axis=1)
    for slot in range(CAP):
        reach = (slot + 1) * half
        span = slice(slot * half, reach)
        keys = k_ref[:reach, :]
        present = row_seg_ref[span, :] >= 0
        for head in range(QPK):
            cols = slice(head * HD, (head + 1) * HD)
            scores = lax.dot_general(
                q_ref[span, cols], keys, (((1,), (1,)), ((), ())),
                preferred_element_type=jnp.float32,
            )
            scores = scores + bias_ref[span, :reach]
            top = jnp.max(scores, axis=1, keepdims=True)
            raised = jnp.exp2((scores - top) * factor).astype(jnp.bfloat16)
            mixed = jnp.dot(raised, v_wide[:reach], preferred_element_type=jnp.float32)
            result = mixed[:, :HD] / mixed[:, HD:]
            out_ref[span, cols] = jnp.where(present, result, 0.0).astype(jnp.bfloat16)


def attend(slot_queries, slot_kv, slot_segment):
    rows = slot_queries.shape[0]
    width = QPK * HD
    return pl.pallas_call(
        attention_kernel,
        out_shape=jax.ShapeDtypeStruct(slot_queries.shape, jnp.bfloat16),
        grid=(KVH,),
        in_specs=[
            pl.BlockSpec((rows, 1), lambda g: (0, 0)),
            pl.BlockSpec((1, rows), lambda g: (0, 0)),
            pl.BlockSpec((rows, width), lambda g: (0, g)),
            pl.BlockSpec((rows, HD), lambda g: (0, g)),
            pl.BlockSpec((rows, HD), lambda g: (0, KVH + g)),
        ],
        out_specs=pl.BlockSpec((rows, width), lambda g: (0, g)),
        scratch_shapes=[pltpu.VMEM((rows, rows), jnp.float32)],
        compiler_params=pltpu.CompilerParams(vmem_limit_bytes=32 * 1024 * 1024),
    )(slot_segment[:, None], slot_segment[None, :], slot_queries, slot_kv, slot_kv)


def per_device(
    hidden,
    queries,
    segment,
    target_device,
    target_slot,
    key_codes,
    key_scales,
    value_codes,
    value_scales,
):
    local_weights = jnp.concatenate(
        (dequantize(key_codes, key_scales), dequantize(value_codes, value_scales)), axis=1
    )
    depth = local_weights.shape[0]
    block_rows = hidden.shape[0]
    cycle_size = lax.axis_size("shard")
    core = lax.axis_index("shard") % 2
    pairs = [(i, i ^ 1) for i in range(cycle_size)]
    same_core = [list(range(c, cycle_size, 2)) for c in range(2)]
    weights = lax.all_gather(
        local_weights, "shard", axis=0, tiled=True, axis_index_groups=same_core
    )
    columns = hidden.reshape(block_rows, cycle_size // 2, 2, depth)
    kept = lax.dynamic_index_in_dim(columns, core, 2, keepdims=False).reshape(block_rows, -1)
    given = lax.dynamic_index_in_dim(columns, 1 - core, 2, keepdims=False).reshape(block_rows, -1)
    taken = lax.ppermute(given, "shard", pairs)
    slot_segment = slot_segments(segment, target_device, target_slot)
    slot_queries = regroup(queries, target_device, target_slot)
    partial = projector(jnp.concatenate((kept, taken), axis=0), weights)
    other = lax.ppermute(partial[block_rows:], "shard", pairs)
    key_value = (partial[:block_rows] + other).astype(jnp.bfloat16)
    slot_kv = regroup(key_value, target_device, target_slot)
    return attend(slot_queries, slot_kv, slot_segment)


def solution(mesh):
    return jax.shard_map(
        per_device,
        mesh=mesh,
        in_specs=(
            P(("groups", "shard"), None),
            P(("groups", "shard"), None),
            P("groups"),
            P("groups"),
            P("groups"),
            P("shard", None),
            P("shard", None),
            P("shard", None),
            P("shard", None),
        ),
        out_specs=P(("groups", "shard"), None),
        check_vma=False,
    )
```

```python
import functools

import jax
import jax.numpy as jnp
from jax import lax
from jax.experimental import pallas as pl
from jax.experimental.pallas import tpu as pltpu
from jax.sharding import PartitionSpec as P

KVH = 4
HD = 128
QPK = 8
QB = 128
CAP = 2
HOP = 1
TILE = 256
MESH = pl.DeviceIdType.MESH
LOG2E = 1.4426950408889634


def slot_segments(segment, target_device, target_slot):
    own_index = lax.axis_index("shard")
    block_count = target_device.shape[0]
    segment_rows = segment.reshape(block_count, -1)
    matches = jnp.logical_and(
        target_device[:, None] == own_index,
        target_slot[:, None] == jnp.arange(CAP, dtype=jnp.int32)[None, :],
    )
    summed = jnp.sum(jnp.where(matches[:, :, None], segment_rows[:, None, :], 0), axis=0)
    present = jnp.any(matches, axis=0)
    return jnp.where(present[:, None], summed, -1).reshape(-1)


def ring_chip(place, chips, snake):
    if not snake:
        return place
    turned = place // (chips // 2)
    level = (1 - turned) * place + turned * (chips - 1 - place)
    return 2 * level + turned


def ring_place(chip, chips, snake):
    if not snake:
        return chip
    level, side = chip // 2, chip % 2
    return (1 - side) * level + side * (chips - 1 - level)


def row_parts(start, count):
    first = (count // 2 + 15) // 16 * 16
    return ((start, first), (start + first, count - first))


def gather_kernel(
    chips, snake,
    hidden_ref, queries_ref, key_codes_ref, value_codes_ref, key_scales_ref, value_scales_ref,
    q3_ref, kv3_ref,
    weights, rows_in, total, half_in, kv,
    own_sem, give_send, take_sem, up_send, up_recv, down_send, down_recv, x_send, x_recv,
    half_send, half_recv, move_send, move_recv, keep_sem,
):
    block_rows = hidden_ref.shape[0]
    depth, key_width = key_codes_ref.shape
    third = (depth // 3 + 8) // 16 * 16
    shards = 2 * chips
    group = lax.axis_index("groups")
    shard = lax.axis_index("shard")
    chip, core = shard // 2, shard % 2
    place = ring_place(chip, chips, snake)
    x_side = group % 2

    def ids(group_id, shard_id):
        return {"groups": group_id, "shard": shard_id}

    def on_ring(offset):
        return ring_chip((place + offset + chips) % chips, chips, snake)

    up = ids(group, on_ring(1) * 2 + core)
    down = ids(group, on_ring(-1) * 2 + core)
    across = ids(group + 1 - 2 * x_side, shard)
    sibling = ids(group, chip * 2 + 1 - core)
    right = ids(group, (shard + 1) % shards)
    left = ids(group, (shard + shards - 1) % shards)

    def remote(src, dst, send, recv, device):
        return pltpu.make_async_remote_copy(
            src_ref=src, dst_ref=dst, send_sem=send, recv_sem=recv,
            device_id=device, device_id_type=MESH,
        )

    barrier = pltpu.get_barrier_semaphore()
    for device in (up, down, across, right, left):
        pl.semaphore_signal(barrier, inc=1, device_id=device, device_id_type=MESH)

    local = []
    for m in range(chips):
        columns = pl.ds(pl.multiple_of((2 * m + core) * depth, 128), depth)
        local.append(pltpu.make_async_copy(
            hidden_ref.at[:, columns], rows_in.at[m, pl.ds(0, block_rows)], own_sem.at[m]
        ))
        local[-1].start()
    keep_q = pltpu.make_async_copy(queries_ref, q3_ref.at[0], keep_sem.at[0])
    keep_q.start()

    for codes_ref, scales_ref, base in (
        (key_codes_ref, key_scales_ref, 0), (value_codes_ref, value_scales_ref, key_width)
    ):
        for i in range(depth // QB):
            for j in range(key_width // QB):
                block = codes_ref[i * QB:(i + 1) * QB, j * QB:(j + 1) * QB].astype(jnp.float32)
                weights[chip, i * QB:(i + 1) * QB, base + j * QB:base + (j + 1) * QB] = (
                    block * scales_ref[i, j]
                ).astype(jnp.bfloat16)

    pl.semaphore_wait(barrier, 5)

    mine = row_parts(x_side * (depth - third), third)
    theirs = row_parts((1 - x_side) * (depth - third), third)
    shared = row_parts(third, depth - 2 * third)

    def piece(owner, part):
        return weights.at[owner, pl.ds(pl.multiple_of(part[0], 16), part[1])]

    sends = []

    def pass_up(step, sub, owner):
        ref = piece(owner, mine[sub])
        copy = remote(ref, ref, up_send.at[step, sub], up_recv.at[step, sub], up)
        copy.start()
        sends.append(copy)

    def pass_down(step, sub, owner):
        ref = piece(owner, shared[sub])
        copy = remote(ref, ref, down_send.at[step, sub], down_recv.at[step, sub], down)
        copy.start()
        sends.append(copy)

    def pass_across(step, sub, owner):
        ref = piece(owner, mine[sub])
        copy = remote(ref, ref, x_send.at[step, sub], x_recv.at[step, sub], across)
        copy.start()
        sends.append(copy)

    for sub in range(2):
        pass_up(0, sub, chip)
        pass_down(0, sub, chip)

    given = []
    for m in range(chips):
        columns = pl.ds(pl.multiple_of((2 * m + 1 - core) * depth, 128), depth)
        given.append(remote(
            hidden_ref.at[:, columns], rows_in.at[m, pl.ds(block_rows, block_rows)],
            give_send.at[m], take_sem.at[m], sibling,
        ))
        given[-1].start()

    moves = [
        remote(queries_ref, q3_ref.at[1], move_send.at[0], move_recv.at[0], right),
        remote(queries_ref, q3_ref.at[2], move_send.at[1], move_recv.at[1], left),
    ]
    for move in moves:
        move.start()

    def multiply(owner, first):
        @pl.loop(0, 2 * key_width // TILE)
        def _(t):
            columns = pl.ds(pl.multiple_of(t * TILE, TILE), TILE)
            product = jnp.dot(
                rows_in[owner], weights[owner, :, columns], preferred_element_type=jnp.float32
            )
            if first:
                total[:, columns] = product
            else:
                total[:, columns] += product

    def finish(back):
        owner = on_ring(-back)
        for sub in range(2):
            ref = piece(owner, theirs[sub])
            remote(
                ref, ref, x_send.at[back - 1, sub], x_recv.at[back - 1, sub], across
            ).wait_recv()
        multiply(owner, False)

    for step in range(1, chips):
        behind, ahead = on_ring(-step), on_ring(step)
        for sub in range(2):
            ref = piece(behind, mine[sub])
            remote(
                ref, ref, up_send.at[step - 1, sub], up_recv.at[step - 1, sub], up
            ).wait_recv()
            if step < chips - 1:
                pass_up(step, sub, behind)
            pass_across(step - 1, sub, behind)
            ref = piece(ahead, shared[sub])
            remote(
                ref, ref, down_send.at[step - 1, sub], down_recv.at[step - 1, sub], down
            ).wait_recv()
            if step < chips - 1:
                pass_down(step, sub, ahead)
        if step == 1:
            for m in range(chips):
                local[m].wait()
                given[m].wait()
            multiply(chip, True)
        for back in range(1, chips):
            if max(back, chips - back) == step - 1:
                finish(back)
    for back in range(1, chips):
        if max(back, chips - back) == chips - 1:
            finish(back)

    half = remote(
        total.at[pl.ds(block_rows, block_rows)], half_in, half_send, half_recv, sibling
    )
    half.start()
    half.wait()
    kv[...] = (total[:block_rows] + half_in[...]).astype(jnp.bfloat16)
    moves.append(remote(kv, kv3_ref.at[1], move_send.at[2], move_recv.at[2], right))
    moves.append(remote(kv, kv3_ref.at[2], move_send.at[3], move_recv.at[3], left))
    for move in moves[2:]:
        move.start()
    keep_kv = pltpu.make_async_copy(kv, kv3_ref.at[0], keep_sem.at[1])
    keep_kv.start()
    for copy in sends:
        copy.wait_send()
    for move in moves:
        move.wait()
    keep_q.wait()
    keep_kv.wait()


def gather_project(mesh_shape, hidden, queries, key_codes, key_scales, value_codes, value_scales):
    block_rows = hidden.shape[0]
    depth, key_width = key_codes.shape
    chips = mesh_shape["shard"] // 2
    snake = mesh_shape["groups"] == 2
    dma = pltpu.SemaphoreType.DMA
    any_space = pl.BlockSpec(memory_space=pl.ANY)
    vmem = pl.BlockSpec(memory_space=pltpu.VMEM)
    smem = pl.BlockSpec(memory_space=pltpu.SMEM)
    steps = (chips - 1, 2)
    return pl.pallas_call(
        functools.partial(gather_kernel, chips, snake),
        out_shape=(
            jax.ShapeDtypeStruct((3,) + queries.shape, jnp.bfloat16),
            jax.ShapeDtypeStruct((3, block_rows, 2 * key_width), jnp.bfloat16),
        ),
        in_specs=[any_space, any_space, vmem, vmem, smem, smem],
        out_specs=(any_space, any_space),
        scratch_shapes=[
            pltpu.VMEM((chips, depth, 2 * key_width), jnp.bfloat16),
            pltpu.VMEM((chips, 2 * block_rows, depth), jnp.bfloat16),
            pltpu.VMEM((2 * block_rows, 2 * key_width), jnp.float32),
            pltpu.VMEM((block_rows, 2 * key_width), jnp.float32),
            pltpu.VMEM((block_rows, 2 * key_width), jnp.bfloat16),
            dma((chips,)), dma((chips,)), dma((chips,)),
            dma(steps), dma(steps), dma(steps), dma(steps), dma(steps), dma(steps),
            dma, dma, dma((4,)), dma((4,)), dma((2,)),
        ],
        compiler_params=pltpu.CompilerParams(
            collective_id=0, has_side_effects=True, vmem_limit_bytes=40 * 1024 * 1024
        ),
        cost_estimate=pl.CostEstimate(
            flops=4 * block_rows * chips * depth * 2 * key_width,
            bytes_accessed=32 * 1024 * 1024, transcendentals=0,
        ),
    )(hidden, queries, key_codes, value_codes, key_scales, value_scales)


def attention_kernel(
    source_ref, row_seg_ref, col_seg_ref, q0_ref, q1_ref, k0_ref, k1_ref, v0_ref, v1_ref,
    out_ref, bias_ref,
):
    half = q0_ref.shape[1]
    rows = CAP * half
    factor = HD ** (-0.5) * LOG2E

    @pl.when(pl.program_id(0) == 0)
    def _():
        row_index = lax.broadcasted_iota(jnp.int32, (rows, rows), 0)
        col_index = lax.broadcasted_iota(jnp.int32, (rows, rows), 1)
        allowed = jnp.logical_and(row_seg_ref[...] == col_seg_ref[...], col_index <= row_index)
        bias_ref[...] = jnp.where(allowed, 0.0, -1e30)

    ones = jnp.ones((rows, HD), jnp.bfloat16)
    all_keys = jnp.concatenate([k0_ref[0], k1_ref[0]], axis=0)
    v_wide = jnp.concatenate(
        [jnp.concatenate([v0_ref[0], v1_ref[0]], axis=0), ones], axis=1
    )
    for slot, q_ref in enumerate((q0_ref, q1_ref)):
        reach = (slot + 1) * half
        span = slice(slot * half, reach)
        keys = all_keys[:reach]
        present = row_seg_ref[span, :] >= 0
        for head in range(QPK):
            cols = slice(head * HD, (head + 1) * HD)
            scores = lax.dot_general(
                q_ref[0, :, cols], keys, (((1,), (1,)), ((), ())),
                preferred_element_type=jnp.float32,
            )
            scores = scores + bias_ref[span, :reach]
            top = jnp.max(scores, axis=1, keepdims=True)
            raised = jnp.exp2((scores - top) * factor).astype(jnp.bfloat16)
            mixed = jnp.dot(raised, v_wide[:reach], preferred_element_type=jnp.float32)
            result = mixed[:, :HD] / mixed[:, HD:]
            out_ref[span, cols] = jnp.where(present, result, 0.0).astype(jnp.bfloat16)


def attend(sources, q3, kv3, slot_segment):
    half = q3.shape[1]
    rows = CAP * half
    width = QPK * HD

    def chosen(slot, base, size):
        return pl.BlockSpec((1, half, size), lambda g, src: (src[slot], 0, base + g))

    return pl.pallas_call(
        attention_kernel,
        out_shape=jax.ShapeDtypeStruct((rows, q3.shape[2]), jnp.bfloat16),
        grid_spec=pltpu.PrefetchScalarGridSpec(
            num_scalar_prefetch=1,
            grid=(KVH,),
            in_specs=[
                pl.BlockSpec((rows, 1), lambda g, src: (0, 0)),
                pl.BlockSpec((1, rows), lambda g, src: (0, 0)),
                chosen(0, 0, width), chosen(1, 0, width),
                chosen(0, 0, HD), chosen(1, 0, HD),
                chosen(0, KVH, HD), chosen(1, KVH, HD),
            ],
            out_specs=pl.BlockSpec((rows, width), lambda g, src: (0, g)),
            scratch_shapes=[pltpu.VMEM((rows, rows), jnp.float32)],
        ),
        compiler_params=pltpu.CompilerParams(vmem_limit_bytes=32 * 1024 * 1024),
    )(sources, slot_segment[:, None], slot_segment[None, :], q3, q3, kv3, kv3, kv3, kv3)


def slot_sources(target_device, target_slot):
    cycle_size = target_device.shape[0]
    own_index = lax.axis_index("shard")
    near = (own_index + jnp.array([0, -1, 1], jnp.int32)) % cycle_size
    lands = target_device[near] == own_index
    hits = jnp.logical_and(
        lands[None, :], target_slot[near][None, :] == jnp.arange(CAP, dtype=jnp.int32)[:, None]
    )
    return jnp.sum(jnp.where(hits, jnp.arange(3, dtype=jnp.int32)[None, :], 0), axis=1)


def per_device(
    mesh_shape,
    hidden,
    queries,
    segment,
    target_device,
    target_slot,
    key_codes,
    key_scales,
    value_codes,
    value_scales,
):
    slot_segment = slot_segments(segment, target_device, target_slot)
    sources = slot_sources(target_device, target_slot)
    q3, kv3 = gather_project(
        mesh_shape, hidden, queries, key_codes, key_scales, value_codes, value_scales
    )
    return attend(sources, q3, kv3, slot_segment)


def solution(mesh):
    return jax.shard_map(
        functools.partial(per_device, dict(mesh.shape)),
        mesh=mesh,
        in_specs=(
            P(("groups", "shard"), None),
            P(("groups", "shard"), None),
            P("groups"),
            P("groups"),
            P("groups"),
            P("shard", None),
            P("shard", None),
            P("shard", None),
            P("shard", None),
        ),
        out_specs=P(("groups", "shard"), None),
        check_vma=False,
    )
```

```python
import functools

import jax
import jax.numpy as jnp
from jax import lax
from jax.experimental import pallas as pl
from jax.experimental.pallas import tpu as pltpu
from jax.sharding import PartitionSpec as P

KVH = 4
HD = 128
QPK = 8
QB = 128
CAP = 2
HOP = 1
TILE = 256
MESH = pl.DeviceIdType.MESH
LOG2E = 1.4426950408889634


def ring_chip(place, chips, snake):
    if not snake:
        return place
    turned = place // (chips // 2)
    level = (1 - turned) * place + turned * (chips - 1 - place)
    return 2 * level + turned


def ring_place(chip, chips, snake):
    if not snake:
        return chip
    level, side = chip // 2, chip % 2
    return (1 - side) * level + side * (chips - 1 - level)


def row_parts(start, count):
    first = (count // 2 + 15) // 16 * 16
    return ((start, first), (start + first, count - first))


def gather_kernel(
    chips, snake,
    hidden_ref, queries_ref, key_codes_ref, value_codes_ref, key_scales_ref, value_scales_ref,
    q3_ref, kv3_ref,
    weights, rows_in, total, half_in, kv,
    own_sem, give_send, take_sem, up_send, up_recv, down_send, down_recv, x_send, x_recv,
    half_send, half_recv, kv_send, kv_recv, move_send, move_recv, keep_sem,
):
    block_rows = hidden_ref.shape[0]
    depth, key_width = key_codes_ref.shape
    quarter = depth // 4
    shards = 2 * chips
    group = lax.axis_index("groups")
    shard = lax.axis_index("shard")
    chip, core = shard // 2, shard % 2
    place = ring_place(chip, chips, snake)
    x_side = group % 2

    def ids(group_id, shard_id):
        return {"groups": group_id, "shard": shard_id}

    def on_ring(offset):
        return ring_chip((place + offset + chips) % chips, chips, snake)

    up = ids(group, on_ring(1) * 2 + core)
    down = ids(group, on_ring(-1) * 2 + core)
    across = ids(group + 1 - 2 * x_side, shard)
    sibling = ids(group, chip * 2 + 1 - core)
    right = ids(group, (shard + 1) % shards)
    left = ids(group, (shard + shards - 1) % shards)

    def remote(src, dst, send, recv, device):
        return pltpu.make_async_remote_copy(
            src_ref=src, dst_ref=dst, send_sem=send, recv_sem=recv,
            device_id=device, device_id_type=MESH,
        )

    barrier = pltpu.get_barrier_semaphore()
    for device in (up, down, across, right, left):
        pl.semaphore_signal(barrier, inc=1, device_id=device, device_id_type=MESH)

    local = []
    for m in range(chips):
        columns = pl.ds(pl.multiple_of((2 * m + core) * depth, 128), depth)
        local.append(pltpu.make_async_copy(
            hidden_ref.at[:, columns], rows_in.at[m, pl.ds(0, block_rows)], own_sem.at[m]
        ))
        local[-1].start()
    keep_q = pltpu.make_async_copy(queries_ref, q3_ref.at[0], keep_sem.at[0])
    keep_q.start()

    for codes_ref, scales_ref, base in (
        (key_codes_ref, key_scales_ref, 0), (value_codes_ref, value_scales_ref, key_width)
    ):
        for i in range(depth // QB):
            for j in range(key_width // QB):
                block = codes_ref[i * QB:(i + 1) * QB, j * QB:(j + 1) * QB].astype(jnp.float32)
                weights[chip, i * QB:(i + 1) * QB, base + j * QB:base + (j + 1) * QB] = (
                    block * scales_ref[i, j]
                ).astype(jnp.bfloat16)

    pl.semaphore_wait(barrier, 5)

    mine_up = row_parts(x_side * 2 * quarter, quarter)
    mine_down = row_parts(x_side * 2 * quarter + quarter, quarter)
    theirs_up = row_parts((1 - x_side) * 2 * quarter, quarter)
    theirs_down = row_parts((1 - x_side) * 2 * quarter + quarter, quarter)

    def piece(owner, part):
        return weights.at[owner, pl.ds(pl.multiple_of(part[0], 16), part[1])]

    sends = []

    def pass_up(step, sub, owner):
        ref = piece(owner, mine_up[sub])
        copy = remote(ref, ref, up_send.at[step, sub], up_recv.at[step, sub], up)
        copy.start()
        sends.append(copy)

    def pass_down(step, sub, owner):
        ref = piece(owner, mine_down[sub])
        copy = remote(ref, ref, down_send.at[step, sub], down_recv.at[step, sub], down)
        copy.start()
        sends.append(copy)

    def pass_across(step, way, sub, owner):
        ref = piece(owner, (mine_up, mine_down)[way][sub])
        copy = remote(ref, ref, x_send.at[step, way, sub], x_recv.at[step, way, sub], across)
        copy.start()
        sends.append(copy)

    for sub in range(2):
        pass_up(0, sub, chip)
        pass_down(0, sub, chip)

    given = []
    for m in range(chips):
        columns = pl.ds(pl.multiple_of((2 * m + 1 - core) * depth, 128), depth)
        given.append(remote(
            hidden_ref.at[:, columns], rows_in.at[m, pl.ds(block_rows, block_rows)],
            give_send.at[m], take_sem.at[m], sibling,
        ))
        given[-1].start()

    moves = [
        remote(queries_ref, q3_ref.at[1], move_send.at[0], move_recv.at[0], right),
        remote(queries_ref, q3_ref.at[2], move_send.at[1], move_recv.at[1], left),
    ]
    for move in moves:
        move.start()

    def multiply(owner, first):
        @pl.loop(0, 2 * key_width // TILE)
        def _(t):
            columns = pl.ds(pl.multiple_of(t * TILE, TILE), TILE)
            product = jnp.dot(
                rows_in[owner], weights[owner, :, columns], preferred_element_type=jnp.float32
            )
            if first:
                total[:, columns] = product
            else:
                total[:, columns] += product

    def complete(back):
        owner = on_ring(-back)
        for way, step in ((0, back - 1), (1, chips - back - 1)):
            for sub in range(2):
                ref = piece(owner, (theirs_up, theirs_down)[way][sub])
                remote(
                    ref, ref, x_send.at[step, way, sub], x_recv.at[step, way, sub], across
                ).wait_recv()
        return owner

    for step in range(1, chips):
        behind, ahead = on_ring(-step), on_ring(step)
        for sub in range(2):
            ref = piece(behind, mine_up[sub])
            remote(
                ref, ref, up_send.at[step - 1, sub], up_recv.at[step - 1, sub], up
            ).wait_recv()
            if step < chips - 1:
                pass_up(step, sub, behind)
            pass_across(step - 1, 0, sub, behind)
            ref = piece(ahead, mine_down[sub])
            remote(
                ref, ref, down_send.at[step - 1, sub], down_recv.at[step - 1, sub], down
            ).wait_recv()
            if step < chips - 1:
                pass_down(step, sub, ahead)
            pass_across(step - 1, 1, sub, ahead)
        if step == 1:
            for m in range(chips):
                local[m].wait()
                given[m].wait()
            multiply(chip, True)
        for back in range(1, chips):
            if max(back, chips - back) == step - 1:
                multiply(complete(back), False)
    owners = [
        complete(back) for back in range(1, chips) if max(back, chips - back) == chips - 1
    ]
    tiles = [pl.ds(t * TILE, TILE) for t in range(2 * key_width // TILE)]
    halves = []
    for t, columns in enumerate(tiles):
        product = total[:, columns]
        for owner in owners:
            product += jnp.dot(
                rows_in[owner], weights[owner, :, columns], preferred_element_type=jnp.float32
            )
        total[:, columns] = product
        halves.append(remote(
            total.at[pl.ds(block_rows, block_rows), columns], half_in.at[:, columns],
            half_send.at[t], half_recv.at[t], sibling,
        ))
        halves[-1].start()
    for t, columns in enumerate(tiles):
        halves[t].wait_recv()
        kv[:, columns] = (total[:block_rows, columns] + half_in[:, columns]).astype(jnp.bfloat16)
        for way, device in ((0, right), (1, left)):
            moves.append(remote(
                kv.at[:, columns], kv3_ref.at[1 + way, :, columns],
                kv_send.at[way, t], kv_recv.at[way, t], device,
            ))
            moves[-1].start()
    keep_kv = pltpu.make_async_copy(kv, kv3_ref.at[0], keep_sem.at[1])
    keep_kv.start()
    for copy in sends + halves:
        copy.wait_send()
    for move in moves:
        move.wait()
    keep_q.wait()
    keep_kv.wait()


def gather_project(mesh_shape, hidden, queries, key_codes, key_scales, value_codes, value_scales):
    block_rows = hidden.shape[0]
    depth, key_width = key_codes.shape
    chips = mesh_shape["shard"] // 2
    snake = mesh_shape["groups"] == 2
    dma = pltpu.SemaphoreType.DMA
    any_space = pl.BlockSpec(memory_space=pl.ANY)
    vmem = pl.BlockSpec(memory_space=pltpu.VMEM)
    smem = pl.BlockSpec(memory_space=pltpu.SMEM)
    steps = (chips - 1, 2)
    tile_count = 2 * key_width // TILE
    return pl.pallas_call(
        functools.partial(gather_kernel, chips, snake),
        out_shape=(
            jax.ShapeDtypeStruct((3,) + queries.shape, jnp.bfloat16),
            jax.ShapeDtypeStruct((3, block_rows, 2 * key_width), jnp.bfloat16),
        ),
        in_specs=[any_space, any_space, vmem, vmem, smem, smem],
        out_specs=(any_space, any_space),
        scratch_shapes=[
            pltpu.VMEM((chips, depth, 2 * key_width), jnp.bfloat16),
            pltpu.VMEM((chips, 2 * block_rows, depth), jnp.bfloat16),
            pltpu.VMEM((2 * block_rows, 2 * key_width), jnp.float32),
            pltpu.VMEM((block_rows, 2 * key_width), jnp.float32),
            pltpu.VMEM((block_rows, 2 * key_width), jnp.bfloat16),
            dma((chips,)), dma((chips,)), dma((chips,)),
            dma(steps), dma(steps), dma(steps), dma(steps),
            dma((chips - 1, 2, 2)), dma((chips - 1, 2, 2)),
            dma((tile_count,)), dma((tile_count,)), dma((2, tile_count)), dma((2, tile_count)),
            dma((2,)), dma((2,)), dma((2,)),
        ],
        compiler_params=pltpu.CompilerParams(
            collective_id=0, has_side_effects=True, vmem_limit_bytes=60 * 1024 * 1024
        ),
        cost_estimate=pl.CostEstimate(
            flops=4 * block_rows * chips * depth * 2 * key_width,
            bytes_accessed=32 * 1024 * 1024, transcendentals=0,
        ),
    )(hidden, queries, key_codes, value_codes, key_scales, value_scales)


def slot_source(slot, own_ref, device_ref, slot_ref, blocks):
    own = own_ref[0]
    source, present = jnp.int32(0), False
    for code, offset in enumerate((0, -1, 1)):
        near = (own + offset + blocks) % blocks
        hit = jnp.logical_and(device_ref[near] == own, slot_ref[near] == slot)
        source = jnp.where(hit, code, source)
        present = jnp.logical_or(present, hit)
    return source, present


def attention_kernel(
    blocks, own_ref, device_ref, slot_ref,
    s0_ref, s1_ref, q0_ref, q1_ref, k0_ref, k1_ref, v0_ref, v1_ref, out_ref, bias_ref,
):
    half = q0_ref.shape[1]
    rows = CAP * half
    factor = HD ** (-0.5) * LOG2E
    present = [slot_source(s, own_ref, device_ref, slot_ref, blocks)[1] for s in range(CAP)]

    @pl.when(pl.program_id(0) == 0)
    def _():
        row_index = lax.broadcasted_iota(jnp.int32, (rows, rows), 0)
        col_index = lax.broadcasted_iota(jnp.int32, (rows, rows), 1)
        ids = jnp.concatenate(
            [
                jnp.where(present[0], s0_ref[0].astype(jnp.float32), -1.0),
                jnp.where(present[1], s1_ref[0].astype(jnp.float32), -1.0),
            ],
            axis=1,
        )
        turned = jnp.transpose(jnp.broadcast_to(ids, (HD, rows)))[:, :1]
        allowed = jnp.logical_and(turned == ids, col_index <= row_index)
        bias_ref[...] = jnp.where(allowed, 0.0, -1e30)

    ones = jnp.ones((rows, HD), jnp.bfloat16)
    all_keys = jnp.concatenate([k0_ref[0], k1_ref[0]], axis=0)
    v_wide = jnp.concatenate(
        [jnp.concatenate([v0_ref[0], v1_ref[0]], axis=0), ones], axis=1
    )

    def fill(slot, q_ref):
        reach = (slot + 1) * half
        span = slice(slot * half, reach)
        keys = all_keys[:reach]
        for head in range(QPK):
            cols = slice(head * HD, (head + 1) * HD)
            scores = lax.dot_general(
                q_ref[0, :, cols], keys, (((1,), (1,)), ((), ())),
                preferred_element_type=jnp.float32,
            )
            scores = scores + bias_ref[span, :reach]
            top = jnp.max(scores, axis=1, keepdims=True)
            raised = jnp.exp2((scores - top) * factor).astype(jnp.bfloat16)
            mixed = jnp.dot(raised, v_wide[:reach], preferred_element_type=jnp.float32)
            out_ref[span, cols] = (mixed[:, :HD] / mixed[:, HD:]).astype(jnp.bfloat16)

    for slot, q_ref in enumerate((q0_ref, q1_ref)):
        @pl.when(present[slot])
        def _():
            fill(slot, q_ref)

        @pl.when(jnp.logical_not(present[slot]))
        def _():
            out_ref[slot * half:(slot + 1) * half, :] = jnp.zeros(
                (half, out_ref.shape[1]), jnp.bfloat16
            )


def attend(target_device, target_slot, segment, q3, kv3):
    half = q3.shape[1]
    rows = CAP * half
    width = QPK * HD
    blocks = target_device.shape[0]
    own = lax.axis_index("shard").astype(jnp.int32).reshape(1)

    def chosen(slot, base, size):
        return pl.BlockSpec(
            (1, half, size),
            lambda g, *scalars: (slot_source(slot, *scalars, blocks)[0], 0, base + g),
        )

    def chosen_ids(slot):
        def place(g, *scalars):
            source = slot_source(slot, *scalars, blocks)[0]
            shift = jnp.where(source == 1, blocks - 1, jnp.where(source == 2, 1, 0))
            return ((scalars[0][0] + shift) % blocks, 0, 0)
        return pl.BlockSpec((1, 1, half), place)

    return pl.pallas_call(
        functools.partial(attention_kernel, blocks),
        out_shape=jax.ShapeDtypeStruct((rows, q3.shape[2]), jnp.bfloat16),
        grid_spec=pltpu.PrefetchScalarGridSpec(
            num_scalar_prefetch=3,
            grid=(KVH,),
            in_specs=[
                chosen_ids(0), chosen_ids(1),
                chosen(0, 0, width), chosen(1, 0, width),
                chosen(0, 0, HD), chosen(1, 0, HD),
                chosen(0, KVH, HD), chosen(1, KVH, HD),
            ],
            out_specs=pl.BlockSpec((rows, width), lambda g, *scalars: (0, g)),
            scratch_shapes=[pltpu.VMEM((rows, rows), jnp.float32)],
        ),
        compiler_params=pltpu.CompilerParams(vmem_limit_bytes=60 * 1024 * 1024),
    )(own, target_device, target_slot, segment.reshape(blocks, 1, half), segment.reshape(blocks, 1, half), q3, q3, kv3, kv3, kv3, kv3)


def per_device(
    mesh_shape,
    hidden,
    queries,
    segment,
    target_device,
    target_slot,
    key_codes,
    key_scales,
    value_codes,
    value_scales,
):
    q3, kv3 = gather_project(
        mesh_shape, hidden, queries, key_codes, key_scales, value_codes, value_scales
    )
    return attend(target_device, target_slot, segment, q3, kv3)


def solution(mesh):
    return jax.shard_map(
        functools.partial(per_device, dict(mesh.shape)),
        mesh=mesh,
        in_specs=(
            P(("groups", "shard"), None),
            P(("groups", "shard"), None),
            P("groups"),
            P("groups"),
            P("groups"),
            P("shard", None),
            P("shard", None),
            P("shard", None),
            P("shard", None),
        ),
        out_specs=P(("groups", "shard"), None),
        check_vma=False,
    )
```
